32 devices in a mesh: pole: 2 (over y), row: 4 (over z), col: 2 (over x), sub: 2 (over core).
Axes of the slice: x: 2, y: 2, z: 4, core: 2. Of those that a mesh axis runs over, the one named last changes fastest.
Arguments:
- ancestor_inv: float32 [16384, 8192], P(('pole', 'row'), 'col'), parts along dimension 0
- lower_hat: float32 [6144, 2048], P(('pole', 'row')), parts along dimension 0, may hold values from -2 to 2
- diag_term: float32 [4096, 2048], P(('pole', 'row'), ('col', 'sub')), parts along dimension 0, may hold values from -6 to 6
- row_blocks: int32 [12], replicated, may hold values from 0 to 31, as said below
Outputs:
- offdiag_inv: float32 [16384, 2048], P(('pole', 'row'), ('col', 'sub')), parts along dimension 0
- diag_inv: float32 [4096, 2048], P(('pole', 'row'), ('col', 'sub')), parts along dimension 0
The draws below stay inside these ranges and needn't reach their ends.
There are 2 independent parts, one for each index of `pole`. The reference program is written for one: setup_inputs(seed, part) draws one part's arguments, and reference() takes and returns one part's arrays. A program takes and returns all parts, laid end to end along the dimension named above; an argument that names none is the same for every part. Nothing has to cross between parts.
Inputs may be any that keep to these rules, and one draw needn't show every extreme that they name: `row_blocks`: 12 distinct ancestor block indices in increasing order; the last is always 32 - 1, the root's block.
All inputs are finite; a program needn't handle non-finite values.
Results may differ from the reference program's by a relative error of at most 0.000071.
Values sent between devices are 32-bit elements; how exact they have to be, the bound alone decides.
A program may use at most 192 MiB of HBM per device.

```python
import math
import jax
import jax.numpy as jnp
from jax import lax

TILE = 256
SCOLS = 2048
NAT = 32
RB = 12
RSEL = 3072


def draw_ancestor_inv(key, part):
    key = jax.random.fold_in(key, 11)
    first_key, second_key = jax.random.split(key)
    order = NAT * TILE
    raw = jax.random.normal(first_key, (order, order), jnp.float32)
    symmetric = (raw + raw.T) * (0.7 / math.sqrt(RB * TILE))
    diagonal = jax.random.uniform(second_key, (order,), jnp.float32, 1.0, 3.0)
    identity = (jnp.arange(order)[:, None] == jnp.arange(order)[None, :]).astype(jnp.float32)
    return symmetric + identity * diagonal[None, :]


def draw_row_blocks(key, part):
    key = jax.random.fold_in(key, 7)
    shuffled = jax.random.permutation(key, NAT - 1)
    picked = jnp.sort(shuffled[:RB - 1])
    return jnp.concatenate([picked, jnp.array([NAT - 1])]).astype(jnp.int32)


def levels(rng, extent, pieces, smallest, top_value):
    level = 1.0
    for axis_at, blocks in pieces:
        draws = jax.random.uniform(jax.random.fold_in(jax.random.fold_in(rng, 6), axis_at), (blocks,), jnp.float32, smallest / len(pieces), top_value / len(pieces))
        level = level * jnp.repeat(jnp.exp(draws), extent[axis_at] // blocks).reshape((-1,) + (1,) * (len(extent) - 1 - axis_at))
    return level


def centred(stream_key, shape, width, most, cuts=(), held_as=jnp.bfloat16):
    entries = width * jax.random.normal(stream_key, shape, jnp.float32)
    if cuts:
        entries = entries * levels(stream_key, shape, cuts, -0.22, 0.18)
    return jnp.clip(entries, -most, most).astype(held_as)


def setup_inputs(seed: int = 0, part: int = 0) -> dict:
    streams_of = jax.random.split(jax.random.key(seed), 5)
    part_splits = jax.random.split(jax.random.fold_in(streams_of[4], part), 5)
    return {
        "ancestor_inv": draw_ancestor_inv(jax.random.fold_in(jax.random.fold_in(streams_of[4], part), 71), part),
        "lower_hat": centred(part_splits[1], (RSEL, SCOLS), 0.15, 2.0, ((0, 4),), jnp.float32),
        "diag_term": centred(part_splits[2], (SCOLS, SCOLS), 0.5, 6.0, ((0, 4), (1, 4)), jnp.float32),
        "row_blocks": draw_row_blocks(jax.random.fold_in(streams_of[4], 71), part),
    }


def reference(ancestor_inv, lower_hat, diag_term, row_blocks):
    offsets = jnp.arange(TILE, dtype=jnp.int32)
    chosen_rows = (row_blocks[:, None] * TILE + offsets[None, :]).reshape(-1).astype(jnp.int32)
    block_rows = jnp.take(ancestor_inv, chosen_rows, axis=0)
    block_sel = jnp.take(block_rows, chosen_rows, axis=1)
    product = jnp.dot(block_sel, lower_hat, precision=lax.Precision.HIGHEST, preferred_element_type=jnp.float32)
    offdiag_inv = jnp.zeros((NAT * TILE, SCOLS), jnp.float32).at[chosen_rows].set(-product)
    diag_inv = diag_term + jnp.dot(lower_hat.T, product, precision=lax.Precision.HIGHEST, preferred_element_type=jnp.float32)
    return offdiag_inv, diag_inv
```

```python
import functools

import jax
import jax.numpy as jnp
from jax import lax
from jax.experimental import pallas as pl
from jax.experimental.pallas import tpu as pltpu
from jax.sharding import PartitionSpec as P

TILE = 256
LEVELS = ((4, 7), (5, 8), (6, 9))
VMEM_LIMIT = 48 * 1024 * 1024


def dot3(left, right, dims):
    left_high = left.astype(jnp.bfloat16)
    left_low = (left - left_high.astype(jnp.float32)).astype(jnp.bfloat16)
    right_high = right.astype(jnp.bfloat16)
    right_low = (right - right_high.astype(jnp.float32)).astype(jnp.bfloat16)

    def dot(one, two):
        return lax.dot_general(one, two, (dims, ((), ())), preferred_element_type=jnp.float32)

    return dot(left_high, right_high) + (dot(left_high, right_low) + dot(left_low, right_high))


def pick_tiles(ancestor_inv, tile_rows, tile_cols, sub_index, n_sub):
    half = TILE // n_sub
    n_rows, n_cols = tile_rows.shape[0], tile_cols.shape[0]

    def kernel(rows_ref, cols_ref, sub_ref, tile_ref, out_ref):
        out_ref[...] = tile_ref[...]

    return pl.pallas_call(
        kernel,
        out_shape=jax.ShapeDtypeStruct((n_rows * half, n_cols * TILE), jnp.float32),
        grid_spec=pltpu.PrefetchScalarGridSpec(
            num_scalar_prefetch=3,
            grid=(n_rows, n_cols),
            in_specs=[
                pl.BlockSpec(
                    (half, TILE),
                    lambda i, j, rows, cols, sub: (rows[i] * n_sub + sub[0], cols[j]),
                )
            ],
            out_specs=pl.BlockSpec((half, TILE), lambda i, j, rows, cols, sub: (i, j)),
        ),
    )(tile_rows, tile_cols, sub_index.reshape(1), ancestor_inv)


def product_rows(picked, lower_full, tile_cell, tile_at, row_valid):
    n_col, n_sub, height, _ = picked.shape
    n_rows = row_valid.shape[0]
    half = TILE // n_sub
    width = lower_full.shape[1]
    n_tiles = tile_cell.shape[0]

    def kernel(cell_ref, at_ref, valid_ref, tile_ref, lower_ref, out_ref, total):
        step = pl.program_id(1)

        @pl.when(step == 0)
        def _():
            total[...] = jnp.zeros_like(total)

        total[...] += dot3(tile_ref[0, 0], lower_ref[...], ((1,), (0,)))

        @pl.when(step == n_tiles - 1)
        def _():
            for k in range(n_rows):
                block = total[k * half:(k + 1) * half, :]
                out_ref[k, 0] = jnp.where(valid_ref[k] > 0, block, 0.0)

    out = pl.pallas_call(
        kernel,
        out_shape=jax.ShapeDtypeStruct((n_rows, n_sub, half, width), jnp.float32),
        grid_spec=pltpu.PrefetchScalarGridSpec(
            num_scalar_prefetch=3,
            grid=(n_sub, n_tiles),
            in_specs=[
                pl.BlockSpec(
                    (1, 1, height, TILE), lambda s, j, cell, at, valid: (cell[j], s, 0, at[j])
                ),
                pl.BlockSpec((TILE, width), lambda s, j, cell, at, valid: (j, 0)),
            ],
            out_specs=pl.BlockSpec(
                (n_rows, 1, half, width), lambda s, j, cell, at, valid: (0, s, 0, 0)
            ),
            scratch_shapes=[pltpu.VMEM((height, width), jnp.float32)],
        ),
        compiler_params=pltpu.CompilerParams(vmem_limit_bytes=VMEM_LIMIT),
        cost_estimate=pl.CostEstimate(
            flops=6 * n_rows * TILE * n_tiles * TILE * width,
            bytes_accessed=4 * n_rows * n_tiles * TILE * TILE,
            transcendentals=0,
        ),
    )(tile_cell, tile_at, row_valid, picked, lower_full)
    return out.reshape(n_rows * TILE, width)


def place_rows(product, tile_source, tile_valid, row_tiles):
    width = product.shape[1]

    def kernel(source_ref, valid_ref, rows_ref, out_ref):
        tile = pl.program_id(0)
        out_ref[...] = jnp.where(valid_ref[tile] > 0, -rows_ref[...], 0.0)

    return pl.pallas_call(
        kernel,
        out_shape=jax.ShapeDtypeStruct((row_tiles * TILE, width), jnp.float32),
        grid_spec=pltpu.PrefetchScalarGridSpec(
            num_scalar_prefetch=2,
            grid=(row_tiles,),
            in_specs=[pl.BlockSpec((TILE, width), lambda t, source, valid: (source[t], 0))],
            out_specs=pl.BlockSpec((TILE, width), lambda t, source, valid: (t, 0)),
        ),
        cost_estimate=pl.CostEstimate(
            flops=0, bytes_accessed=8 * row_tiles * TILE * width, transcendentals=0
        ),
    )(tile_source, tile_valid, product)


def diagonal_partial(lower_cells, product):
    n_cells, depth, width = lower_cells.shape

    def kernel(lower_ref, product_ref, out_ref):
        out_ref[...] = dot3(lower_ref[0], product_ref[...], ((0,), (0,)))

    return pl.pallas_call(
        kernel,
        out_shape=jax.ShapeDtypeStruct((n_cells * width, width), jnp.float32),
        grid=(n_cells,),
        in_specs=[
            pl.BlockSpec((1, depth, width), lambda q: (q, 0, 0)),
            pl.BlockSpec((depth, width), lambda q: (0, 0)),
        ],
        out_specs=pl.BlockSpec((width, width), lambda q: (q, 0)),
        compiler_params=pltpu.CompilerParams(vmem_limit_bytes=VMEM_LIMIT),
        cost_estimate=pl.CostEstimate(
            flops=6 * n_cells * depth * width * width,
            bytes_accessed=4 * n_cells * (depth + width) * width,
            transcendentals=0,
        ),
    )(lower_cells, product)


def level_body(caps, ancestor_inv, lower_hat, diag_term, row_blocks):
    row_cap, col_cap = caps
    n_col, n_sub = lax.axis_size("col"), lax.axis_size("sub")
    col_index = lax.axis_index("col")
    row_index = lax.axis_index("row")
    sub_index = lax.axis_index("sub")
    row_tiles, col_tiles = ancestor_inv.shape[0] // TILE, ancestor_inv.shape[1] // TILE
    n_blocks = row_blocks.shape[0]
    width = lower_hat.shape[1] // (n_col * n_sub)

    row_first = jnp.minimum(jnp.sum(row_blocks < row_index * row_tiles), n_blocks - row_cap)
    row_run = lax.dynamic_slice(row_blocks, (row_first,), (row_cap,))
    row_valid = (row_run // row_tiles == row_index).astype(jnp.int32)
    tile_rows = jnp.clip(row_run - row_index * row_tiles, 0, row_tiles - 1)
    cells = jnp.arange(n_col, dtype=jnp.int32)
    col_firsts = jnp.sum(row_blocks[None, :] < (cells * col_tiles)[:, None], axis=1)
    col_firsts = jnp.minimum(col_firsts, n_blocks - col_cap).astype(jnp.int32)
    col_first = lax.dynamic_index_in_dim(col_firsts, col_index, 0, keepdims=False)
    col_run = lax.dynamic_slice(row_blocks, (col_first,), (col_cap,))
    tile_cols = jnp.clip(col_run - col_index * col_tiles, 0, col_tiles - 1)
    tile_cell = row_blocks // col_tiles
    tile_at = jnp.arange(n_blocks, dtype=jnp.int32) - col_firsts[tile_cell]
    own_tiles = row_index * row_tiles + jnp.arange(row_tiles, dtype=jnp.int32)
    hits = (own_tiles[:, None] == row_run[None, :]).astype(jnp.int32)
    tile_valid = jnp.sum(hits, axis=1)
    tile_source = jnp.sum(hits * jnp.arange(row_cap, dtype=jnp.int32)[None, :], axis=1)

    own = lax.dynamic_slice_in_dim(
        lower_hat, (col_index * n_sub + sub_index) * width, width, axis=1
    )
    lower_full = lax.all_gather(own, "row", axis=0, tiled=True)
    picked = pick_tiles(ancestor_inv, tile_rows, tile_cols, sub_index, n_sub)
    picked = lax.all_gather(picked, "col", axis=0)
    picked = lax.all_gather(picked, "sub", axis=1)
    window = lax.dynamic_slice_in_dim(lower_full, row_first * TILE, row_cap * TILE, axis=0)
    window = lax.all_gather(window, "col", axis=0)
    window = lax.all_gather(window, "sub", axis=1)
    product = product_rows(picked, lower_full, tile_cell, tile_at, row_valid)
    partial_value = diagonal_partial(
        window.reshape(n_col * n_sub, row_cap * TILE, width), product
    )
    reduced = lax.psum_scatter(partial_value, "row", scatter_dimension=0, tiled=True)
    offdiag_inv = place_rows(product, tile_source, tile_valid, row_tiles)
    return (offdiag_inv, diag_term + reduced)


def body(ancestor_inv, lower_hat, diag_term, row_blocks):
    n_row, n_col = lax.axis_size("row"), lax.axis_size("col")
    row_tiles, col_tiles = ancestor_inv.shape[0] // TILE, ancestor_inv.shape[1] // TILE
    most_rows = min(row_tiles, row_blocks.shape[0])
    most_cols = min(col_tiles, row_blocks.shape[0])
    caps = [level for level in LEVELS if level[0] < most_rows and level[1] < most_cols]
    caps.append((most_rows, most_cols))
    in_row = jnp.sum(row_blocks[None, :] // row_tiles == jnp.arange(n_row)[:, None], axis=1)
    in_col = jnp.sum(row_blocks[None, :] // col_tiles == jnp.arange(n_col)[:, None], axis=1)
    needed_rows, needed_cols = jnp.max(in_row), jnp.max(in_col)
    choice = jnp.int32(0)
    for level in caps[:-1]:
        short = (needed_rows > level[0]) | (needed_cols > level[1])
        choice = choice + short.astype(jnp.int32)
    operands = (ancestor_inv, lower_hat, diag_term, row_blocks)
    if len(caps) == 1:
        return level_body(caps[0], *operands)
    return lax.switch(choice, [functools.partial(level_body, level) for level in caps], *operands)


def solution(mesh):
    return jax.shard_map(
        body,
        mesh=mesh,
        in_specs=(
            P(("pole", "row"), "col"),
            P(("pole", "row"), None),
            P(("pole", "row"), ("col", "sub")),
            P(),
        ),
        out_specs=(P(("pole", "row"), ("col", "sub")), P(("pole", "row"), ("col", "sub"))),
        check_vma=False,
    )
```

```python
import functools

import jax
import jax.numpy as jnp
from jax import lax
from jax.experimental import pallas as pl
from jax.experimental.pallas import tpu as pltpu
from jax.sharding import PartitionSpec as P

TILE = 256
LEVELS = ((4, 7), (5, 7), (5, 8), (6, 8), (6, 10))
PARTS = 2
VMEM_LIMIT = 48 * 1024 * 1024


def halves(value):
    high = value.astype(jnp.bfloat16)
    return high, (value - high.astype(jnp.float32)).astype(jnp.bfloat16)


def dot3(left, right, dims):
    (left_high, left_low), (right_high, right_low) = left, right

    def dot(one, two):
        return lax.dot_general(one, two, (dims, ((), ())), preferred_element_type=jnp.float32)

    return dot(left_high, right_high) + (dot(left_high, right_low) + dot(left_low, right_high))


def shift(value, axis, hops):
    size = lax.axis_size(axis)
    return lax.ppermute(value, axis, [(i, (i - hops) % size) for i in range(size)])


def pick_tiles(ancestor_inv, tile_rows, tile_cols):
    n_rows, n_cols = tile_rows.shape[0], tile_cols.shape[0]

    def kernel(rows_ref, cols_ref, *refs):
        for j in range(n_cols):
            refs[-1][:, j * TILE:(j + 1) * TILE] = refs[j][...]

    def tile_spec(j):
        return pl.BlockSpec((TILE, TILE), lambda i, rows, cols: (rows[i], cols[j]))

    return pl.pallas_call(
        kernel,
        out_shape=jax.ShapeDtypeStruct((n_rows * TILE, n_cols * TILE), jnp.float32),
        grid_spec=pltpu.PrefetchScalarGridSpec(
            num_scalar_prefetch=2,
            grid=(n_rows,),
            in_specs=[tile_spec(j) for j in range(n_cols)],
            out_specs=pl.BlockSpec((TILE, n_cols * TILE), lambda i, rows, cols: (i, 0)),
        ),
        compiler_params=pltpu.CompilerParams(vmem_limit_bytes=VMEM_LIMIT),
        cost_estimate=pl.CostEstimate(
            flops=0, bytes_accessed=8 * n_rows * n_cols * TILE * TILE, transcendentals=0
        ),
    )(tile_rows, tile_cols, *[ancestor_inv] * n_cols)


def product_rows(own, remotes, lower_parts, tile_hop, tile_at, piece, half_valid):
    n_sub, n_far = len(remotes), len(remotes[0])
    height = own.shape[0] // n_sub
    n_halves = half_valid.shape[0] // n_sub
    half = height // n_halves
    n_parts, part = len(lower_parts), lower_parts[0].shape[1]
    width = n_parts * part
    n_tiles = tile_hop.shape[0]

    def kernel(hop_ref, at_ref, piece_ref, valid_ref, own_ref, *refs):
        far_refs, lower_refs, out_ref = refs[:-1 - n_parts], refs[-1 - n_parts:-1], refs[-1]
        turn, step = pl.program_id(0), pl.program_id(1)

        @pl.when(step == 0)
        def _():
            out_ref[...] = jnp.zeros_like(out_ref)

        def add(tile_ref):
            tile = halves(tile_ref[...])
            for p, lower_ref in enumerate(lower_refs):
                out_ref[:, p * part:(p + 1) * part] += dot3(
                    tile, halves(lower_ref[...]), ((1,), (0,))
                )

        @pl.when(hop_ref[step] == 0)
        def _():
            add(own_ref)

        for v in range(n_sub):
            for h in range(n_far):
                @pl.when((turn == v) & (hop_ref[step] == h + 1))
                def _(ref=far_refs[v * n_far + h]):
                    add(ref)

        @pl.when(step == n_tiles - 1)
        def _():
            for k in range(n_halves):
                rows = pl.ds(k * half, half)
                valid = valid_ref[piece_ref[turn] * n_halves + k] > 0
                out_ref[rows, :] = jnp.where(valid, out_ref[rows, :], 0.0)

    def far_map(v, h):
        def index(u, j, hop, at, piece, valid):
            return (0, jnp.where((u == v) & (hop[j] == h + 1), at[j], 0))

        return index

    far_specs = [
        pl.BlockSpec((height, TILE), far_map(v, h)) for v in range(n_sub) for h in range(n_far)
    ]
    return pl.pallas_call(
        kernel,
        out_shape=jax.ShapeDtypeStruct((n_sub * height, width), jnp.float32),
        grid_spec=pltpu.PrefetchScalarGridSpec(
            num_scalar_prefetch=4,
            grid=(n_sub, n_tiles),
            in_specs=[
                pl.BlockSpec(
                    (height, TILE),
                    lambda u, j, hop, at, piece, valid: (
                        piece[u], jnp.where(hop[j] == 0, at[j], 0)
                    ),
                ),
                *far_specs,
                *[pl.BlockSpec((TILE, part), lambda u, j, hop, at, piece, valid: (j, 0))]
                * n_parts,
            ],
            out_specs=pl.BlockSpec(
                (height, width), lambda u, j, hop, at, piece, valid: (piece[u], 0)
            ),
        ),
        compiler_params=pltpu.CompilerParams(vmem_limit_bytes=VMEM_LIMIT),
        cost_estimate=pl.CostEstimate(
            flops=6 * n_sub * height * n_tiles * TILE * width,
            bytes_accessed=4 * n_sub * height * n_tiles * TILE,
            transcendentals=0,
        ),
    )(tile_hop, tile_at, piece, half_valid, own, *[r for far in remotes for r in far], *lower_parts)


def place_rows(product, tile_source, tile_valid, row_tiles):
    width = product.shape[1]

    def kernel(source_ref, valid_ref, rows_ref, out_ref):
        tile = pl.program_id(0)
        out_ref[...] = jnp.where(valid_ref[tile] > 0, -rows_ref[...], 0.0)

    return pl.pallas_call(
        kernel,
        out_shape=jax.ShapeDtypeStruct((row_tiles * TILE, width), jnp.float32),
        grid_spec=pltpu.PrefetchScalarGridSpec(
            num_scalar_prefetch=2,
            grid=(row_tiles,),
            in_specs=[pl.BlockSpec((TILE, width), lambda t, source, valid: (source[t], 0))],
            out_specs=pl.BlockSpec((TILE, width), lambda t, source, valid: (t, 0)),
        ),
        cost_estimate=pl.CostEstimate(
            flops=0, bytes_accessed=8 * row_tiles * TILE * width, transcendentals=0
        ),
    )(tile_source, tile_valid, product)


def diagonal_partial(windows, product, order):
    n_cells, n_parts = len(windows), len(windows[0])
    depth, width = product.shape
    part = width // n_parts

    def kernel(order_ref, *refs):
        product_ref, out_ref = refs[-2:]
        product_halves = halves(product_ref[...])
        for q in range(n_cells):
            @pl.when(pl.program_id(0) == q)
            def _(q=q):
                for p in range(n_parts):
                    out_ref[p * part:(p + 1) * part, :] = dot3(
                        halves(refs[q * n_parts + p][...]), product_halves, ((0,), (0,))
                    )

    def whole(columns):
        return pl.BlockSpec(
            (depth, columns), lambda q, order: (0, 0), pipeline_mode=pl.Buffered(1)
        )

    return pl.pallas_call(
        kernel,
        out_shape=jax.ShapeDtypeStruct((n_cells * width, width), jnp.float32),
        grid_spec=pltpu.PrefetchScalarGridSpec(
            num_scalar_prefetch=1,
            grid=(n_cells,),
            in_specs=[whole(part)] * (n_cells * n_parts) + [whole(width)],
            out_specs=pl.BlockSpec((width, width), lambda q, order: (order[q], 0)),
        ),
        compiler_params=pltpu.CompilerParams(vmem_limit_bytes=VMEM_LIMIT),
        cost_estimate=pl.CostEstimate(
            flops=6 * n_cells * depth * width * width,
            bytes_accessed=4 * (n_cells + 1) * depth * width,
            transcendentals=0,
        ),
    )(order, *[w for cell in windows for w in cell], product)


def level_body(caps, ancestor_inv, lower_hat, diag_term, row_blocks):
    row_cap, col_cap = caps
    n_col, n_sub = lax.axis_size("col"), lax.axis_size("sub")
    col_index = lax.axis_index("col")
    row_index = lax.axis_index("row")
    sub_index = lax.axis_index("sub")
    row_tiles, col_tiles = ancestor_inv.shape[0] // TILE, ancestor_inv.shape[1] // TILE
    n_blocks = row_blocks.shape[0]
    width = lower_hat.shape[1] // (n_col * n_sub)
    n_parts = PARTS if width % (PARTS * 128) == 0 else 1
    part = width // n_parts

    row_first = jnp.minimum(jnp.sum(row_blocks < row_index * row_tiles), n_blocks - row_cap)
    row_run = lax.dynamic_slice(row_blocks, (row_first,), (row_cap,))
    row_valid = (row_run // row_tiles == row_index).astype(jnp.int32)
    tile_rows = jnp.clip(row_run - row_index * row_tiles, 0, row_tiles - 1)
    cells = jnp.arange(n_col, dtype=jnp.int32)
    col_firsts = jnp.sum(row_blocks[None, :] < (cells * col_tiles)[:, None], axis=1)
    col_firsts = jnp.minimum(col_firsts, n_blocks - col_cap).astype(jnp.int32)
    col_first = lax.dynamic_index_in_dim(col_firsts, col_index, 0, keepdims=False)
    col_run = lax.dynamic_slice(row_blocks, (col_first,), (col_cap,))
    tile_cols = jnp.clip(col_run - col_index * col_tiles, 0, col_tiles - 1)
    tile_cell = row_blocks // col_tiles
    tile_hop = (tile_cell - col_index + n_col) % n_col
    tile_at = jnp.arange(n_blocks, dtype=jnp.int32) - col_firsts[tile_cell]
    own_tiles = row_index * row_tiles + jnp.arange(row_tiles, dtype=jnp.int32)
    hits = (own_tiles[:, None] == row_run[None, :]).astype(jnp.int32)
    tile_valid = jnp.sum(hits, axis=1)
    tile_source = jnp.sum(hits * jnp.arange(row_cap, dtype=jnp.int32)[None, :], axis=1)
    subs = jnp.arange(n_sub, dtype=jnp.int32)
    piece = (sub_index + subs) % n_sub
    order = jnp.concatenate([((col_index + h) % n_col) * n_sub + piece for h in range(n_col)])

    lower_parts = []
    for p in range(n_parts):
        first = (col_index * n_sub + sub_index) * width + p * part
        own_cols = lax.dynamic_slice_in_dim(lower_hat, first, part, axis=1)
        lower_parts.append(lax.all_gather(own_cols, "row", axis=0, tiled=True))
    own = pick_tiles(ancestor_inv, tile_rows, tile_cols)
    height = row_cap * TILE // n_sub
    sent = lax.dynamic_slice_in_dim(own, sub_index * height, height, axis=0)
    far = [shift(sent, "col", h) for h in range(1, n_col)]
    remotes = [far] + [[shift(f, "sub", v) for f in far] for v in range(1, n_sub)]
    shifted = []
    for lower in lower_parts:
        mine = lax.dynamic_slice_in_dim(lower, row_first * TILE, row_cap * TILE, axis=0)
        shifted.append([mine] + [shift(mine, "col", h) for h in range(1, n_col)])
    half_valid = jnp.repeat(row_valid, n_sub)
    product = product_rows(own, remotes, lower_parts, tile_hop, tile_at, piece, half_valid)
    shifted[-1], product = lax.optimization_barrier((shifted[-1], product))
    windows = [
        [there[h] if v == 0 else shift(there[h], "sub", v) for there in shifted]
        for h in range(n_col)
        for v in range(n_sub)
    ]
    partial_value = diagonal_partial(windows, product, order)
    reduced = lax.psum_scatter(partial_value, "row", scatter_dimension=0, tiled=True)
    offdiag_inv = place_rows(product, tile_source, tile_valid, row_tiles)
    return (offdiag_inv, diag_term + reduced)


def body(ancestor_inv, lower_hat, diag_term, row_blocks):
    n_row, n_col = lax.axis_size("row"), lax.axis_size("col")
    row_tiles, col_tiles = ancestor_inv.shape[0] // TILE, ancestor_inv.shape[1] // TILE
    most_rows = min(row_tiles, row_blocks.shape[0])
    most_cols = min(col_tiles, row_blocks.shape[0])
    caps = [level for level in LEVELS if level[0] < most_rows and level[1] < most_cols]
    caps.append((most_rows, most_cols))
    in_row = jnp.sum(row_blocks[None, :] // row_tiles == jnp.arange(n_row)[:, None], axis=1)
    in_col = jnp.sum(row_blocks[None, :] // col_tiles == jnp.arange(n_col)[:, None], axis=1)
    needed_rows, needed_cols = jnp.max(in_row), jnp.max(in_col)
    fits = [(needed_rows <= rows) & (needed_cols <= cols) for rows, cols in caps]
    choice = jnp.argmax(jnp.stack(fits))
    operands = (ancestor_inv, lower_hat, diag_term, row_blocks)
    if len(caps) == 1:
        return level_body(caps[0], *operands)
    return lax.switch(choice, [functools.partial(level_body, level) for level in caps], *operands)


def solution(mesh):
    return jax.shard_map(
        body,
        mesh=mesh,
        in_specs=(
            P(("pole", "row"), "col"),
            P(("pole", "row"), None),
            P(("pole", "row"), ("col", "sub")),
            P(),
        ),
        out_specs=(P(("pole", "row"), ("col", "sub")), P(("pole", "row"), ("col", "sub"))),
        check_vma=False,
    )
```

```python
import functools

import jax
import jax.numpy as jnp
from jax import lax
from jax.experimental import pallas as pl
from jax.experimental.pallas import tpu as pltpu
from jax.sharding import PartitionSpec as P

TILE = 256
LEVELS = ((4, 7), (5, 7), (5, 8), (6, 8), (6, 10))
PARTS = 2
VMEM_LIMIT = 48 * 1024 * 1024


def halves(value):
    high = value.astype(jnp.bfloat16)
    return high, (value - high.astype(jnp.float32)).astype(jnp.bfloat16)


def dot3(left, right, dims):
    (left_high, left_low), (right_high, right_low) = left, right

    def dot(one, two):
        return lax.dot_general(one, two, (dims, ((), ())), preferred_element_type=jnp.float32)

    return dot(left_high, right_high) + (dot(left_high, right_low) + dot(left_low, right_high))


def shift(value, axis, hops):
    size = lax.axis_size(axis)
    return lax.ppermute(value, axis, [(i, (i - hops) % size) for i in range(size)])


def pick_tiles(ancestor_inv, tile_rows, tile_cols):
    n_rows, n_cols = tile_rows.shape[0], tile_cols.shape[0]

    def kernel(rows_ref, cols_ref, *refs):
        for j in range(n_cols):
            refs[-1][:, j * TILE:(j + 1) * TILE] = refs[j][...]

    def tile_spec(j):
        return pl.BlockSpec((TILE, TILE), lambda i, rows, cols: (rows[i], cols[j]))

    return pl.pallas_call(
        kernel,
        out_shape=jax.ShapeDtypeStruct((n_rows * TILE, n_cols * TILE), jnp.float32),
        grid_spec=pltpu.PrefetchScalarGridSpec(
            num_scalar_prefetch=2,
            grid=(n_rows,),
            in_specs=[tile_spec(j) for j in range(n_cols)],
            out_specs=pl.BlockSpec((TILE, n_cols * TILE), lambda i, rows, cols: (i, 0)),
        ),
        compiler_params=pltpu.CompilerParams(vmem_limit_bytes=VMEM_LIMIT),
        cost_estimate=pl.CostEstimate(
            flops=0, bytes_accessed=8 * n_rows * n_cols * TILE * TILE, transcendentals=0
        ),
    )(tile_rows, tile_cols, *[ancestor_inv] * n_cols)


def product_rows(own, remotes, lower_parts, tile_hop, tile_at, piece, half_valid):
    n_sub, n_far = len(remotes), len(remotes[0])
    height = own.shape[0] // n_sub
    n_halves = half_valid.shape[0] // n_sub
    half = height // n_halves
    n_parts, part = len(lower_parts), lower_parts[0].shape[1]
    width = n_parts * part
    n_tiles = tile_hop.shape[0]

    def kernel(hop_ref, at_ref, piece_ref, valid_ref, own_ref, *refs):
        far_refs, lower_refs, out_ref = refs[:-1 - n_parts], refs[-1 - n_parts:-1], refs[-1]
        turn, step = pl.program_id(0), pl.program_id(1)

        @pl.when(step == 0)
        def _():
            out_ref[...] = jnp.zeros_like(out_ref)

        def add(tile_ref):
            tile = halves(tile_ref[...])
            for p, lower_ref in enumerate(lower_refs):
                out_ref[:, p * part:(p + 1) * part] += dot3(
                    tile, halves(lower_ref[...]), ((1,), (0,))
                )

        @pl.when(hop_ref[step] == 0)
        def _():
            add(own_ref)

        for v in range(n_sub):
            for h in range(n_far):
                @pl.when((turn == v) & (hop_ref[step] == h + 1))
                def _(ref=far_refs[v * n_far + h]):
                    add(ref)

        @pl.when(step == n_tiles - 1)
        def _():
            for k in range(n_halves):
                rows = pl.ds(k * half, half)
                valid = valid_ref[piece_ref[turn] * n_halves + k] > 0
                out_ref[rows, :] = jnp.where(valid, out_ref[rows, :], 0.0)

    def far_map(v, h):
        def index(u, j, hop, at, piece, valid):
            return (0, jnp.where((u == v) & (hop[j] == h + 1), at[j], 0))

        return index

    far_specs = [
        pl.BlockSpec((height, TILE), far_map(v, h)) for v in range(n_sub) for h in range(n_far)
    ]
    return pl.pallas_call(
        kernel,
        out_shape=jax.ShapeDtypeStruct((n_sub * height, width), jnp.float32),
        grid_spec=pltpu.PrefetchScalarGridSpec(
            num_scalar_prefetch=4,
            grid=(n_sub, n_tiles),
            in_specs=[
                pl.BlockSpec(
                    (height, TILE),
                    lambda u, j, hop, at, piece, valid: (
                        piece[u], jnp.where(hop[j] == 0, at[j], 0)
                    ),
                ),
                *far_specs,
                *[pl.BlockSpec((TILE, part), lambda u, j, hop, at, piece, valid: (j, 0))]
                * n_parts,
            ],
            out_specs=pl.BlockSpec(
                (height, width), lambda u, j, hop, at, piece, valid: (piece[u], 0)
            ),
        ),
        compiler_params=pltpu.CompilerParams(vmem_limit_bytes=VMEM_LIMIT),
        cost_estimate=pl.CostEstimate(
            flops=6 * n_sub * height * n_tiles * TILE * width,
            bytes_accessed=4 * n_sub * height * n_tiles * TILE,
            transcendentals=0,
        ),
    )(tile_hop, tile_at, piece, half_valid, own, *[r for far in remotes for r in far], *lower_parts)


def place_rows(products, tile_source, tile_valid, row_tiles):
    width = products[0].shape[1]

    def kernel(source_ref, valid_ref, *refs):
        tile = pl.program_id(0)
        for p, rows_ref in enumerate(refs[:-1]):
            refs[-1][:, p * width:(p + 1) * width] = jnp.where(
                valid_ref[tile] > 0, -rows_ref[...], 0.0
            )

    return pl.pallas_call(
        kernel,
        out_shape=jax.ShapeDtypeStruct((row_tiles * TILE, len(products) * width), jnp.float32),
        grid_spec=pltpu.PrefetchScalarGridSpec(
            num_scalar_prefetch=2,
            grid=(row_tiles,),
            in_specs=[pl.BlockSpec((TILE, width), lambda t, source, valid: (source[t], 0))]
            * len(products),
            out_specs=pl.BlockSpec(
                (TILE, len(products) * width), lambda t, source, valid: (t, 0)
            ),
        ),
        cost_estimate=pl.CostEstimate(
            flops=0, bytes_accessed=8 * row_tiles * TILE * width, transcendentals=0
        ),
    )(tile_source, tile_valid, *products)


def diagonal_partial(windows, products, order):
    n_cells, n_parts = len(windows), len(products)
    depth, height = windows[0].shape
    part = products[0].shape[1]
    width = part * n_parts

    def kernel(order_ref, *refs):
        out_ref, product_refs = refs[-1], refs[-1 - n_parts:-1]
        for q in range(n_cells):
            @pl.when(pl.program_id(0) == q)
            def _(q=q):
                window = halves(refs[q][...])
                for p in range(n_parts):
                    out_ref[:, p * part:(p + 1) * part] = dot3(
                        window, halves(product_refs[p][...]), ((0,), (0,))
                    )

    def whole(columns):
        return pl.BlockSpec(
            (depth, columns), lambda q, order: (0, 0), pipeline_mode=pl.Buffered(1)
        )

    return pl.pallas_call(
        kernel,
        out_shape=jax.ShapeDtypeStruct((n_cells * height, width), jnp.float32),
        grid_spec=pltpu.PrefetchScalarGridSpec(
            num_scalar_prefetch=1,
            grid=(n_cells,),
            in_specs=[whole(height)] * n_cells + [whole(part)] * n_parts,
            out_specs=pl.BlockSpec((height, width), lambda q, order: (order[q], 0)),
        ),
        compiler_params=pltpu.CompilerParams(vmem_limit_bytes=VMEM_LIMIT),
        cost_estimate=pl.CostEstimate(
            flops=6 * n_cells * depth * height * width,
            bytes_accessed=4 * (n_cells + 1) * depth * width,
            transcendentals=0,
        ),
    )(order, *windows, *products)


def level_body(caps, ancestor_inv, lower_hat, diag_term, row_blocks):
    row_cap, col_cap = caps
    n_col, n_sub = lax.axis_size("col"), lax.axis_size("sub")
    col_index = lax.axis_index("col")
    row_index = lax.axis_index("row")
    sub_index = lax.axis_index("sub")
    row_tiles, col_tiles = ancestor_inv.shape[0] // TILE, ancestor_inv.shape[1] // TILE
    n_blocks = row_blocks.shape[0]
    width = lower_hat.shape[1] // (n_col * n_sub)
    one_cell = lax.axis_size("row") == n_col * n_sub
    n_parts = PARTS if one_cell and width % (PARTS * 128) == 0 else 1
    part = width // n_parts

    row_first = jnp.minimum(jnp.sum(row_blocks < row_index * row_tiles), n_blocks - row_cap)
    row_run = lax.dynamic_slice(row_blocks, (row_first,), (row_cap,))
    row_valid = (row_run // row_tiles == row_index).astype(jnp.int32)
    tile_rows = jnp.clip(row_run - row_index * row_tiles, 0, row_tiles - 1)
    cells = jnp.arange(n_col, dtype=jnp.int32)
    col_firsts = jnp.sum(row_blocks[None, :] < (cells * col_tiles)[:, None], axis=1)
    col_firsts = jnp.minimum(col_firsts, n_blocks - col_cap).astype(jnp.int32)
    col_first = lax.dynamic_index_in_dim(col_firsts, col_index, 0, keepdims=False)
    col_run = lax.dynamic_slice(row_blocks, (col_first,), (col_cap,))
    tile_cols = jnp.clip(col_run - col_index * col_tiles, 0, col_tiles - 1)
    tile_cell = row_blocks // col_tiles
    tile_hop = (tile_cell - col_index + n_col) % n_col
    tile_at = jnp.arange(n_blocks, dtype=jnp.int32) - col_firsts[tile_cell]
    own_tiles = row_index * row_tiles + jnp.arange(row_tiles, dtype=jnp.int32)
    hits = (own_tiles[:, None] == row_run[None, :]).astype(jnp.int32)
    tile_valid = jnp.sum(hits, axis=1)
    tile_source = jnp.sum(hits * jnp.arange(row_cap, dtype=jnp.int32)[None, :], axis=1)
    subs = jnp.arange(n_sub, dtype=jnp.int32)
    piece = (sub_index + subs) % n_sub
    order = jnp.concatenate([((col_index + h) % n_col) * n_sub + piece for h in range(n_col)])

    lower_parts = []
    for p in range(n_parts):
        first = (col_index * n_sub + sub_index) * width + p * part
        own_cols = lax.dynamic_slice_in_dim(lower_hat, first, part, axis=1)
        lower_parts.append(lax.all_gather(own_cols, "row", axis=0, tiled=True))
    own = pick_tiles(ancestor_inv, tile_rows, tile_cols)
    height = row_cap * TILE // n_sub
    sent = lax.dynamic_slice_in_dim(own, sub_index * height, height, axis=0)
    far = [shift(sent, "col", h) for h in range(1, n_col)]
    remotes = [far] + [[shift(f, "sub", v) for f in far] for v in range(1, n_sub)]
    shifted = []
    for lower in lower_parts:
        mine = lax.dynamic_slice_in_dim(lower, row_first * TILE, row_cap * TILE, axis=0)
        shifted.append([mine] + [shift(mine, "col", h) for h in range(1, n_col)])
    half_valid = jnp.repeat(row_valid, n_sub)
    products = []
    for p in range(n_parts):
        lower = lower_parts[p]
        if p > 0:
            lower, products[-1] = lax.optimization_barrier((lower, products[-1]))
        products.append(
            product_rows(own, remotes, [lower], tile_hop, tile_at, piece, half_valid)
        )
    shifted[-1], products[-1] = lax.optimization_barrier((shifted[-1], products[-1]))
    reduced = []
    for there in shifted:
        windows = [
            there[h] if v == 0 else shift(there[h], "sub", v)
            for h in range(n_col)
            for v in range(n_sub)
        ]
        partial_value = diagonal_partial(windows, products, order)
        reduced.append(
            lax.psum_scatter(partial_value, "row", scatter_dimension=0, tiled=True)
        )
    offdiag_inv = place_rows(products, tile_source, tile_valid, row_tiles)
    return (offdiag_inv, diag_term + jnp.concatenate(reduced, axis=0))


def body(ancestor_inv, lower_hat, diag_term, row_blocks):
    n_row, n_col = lax.axis_size("row"), lax.axis_size("col")
    row_tiles, col_tiles = ancestor_inv.shape[0] // TILE, ancestor_inv.shape[1] // TILE
    most_rows = min(row_tiles, row_blocks.shape[0])
    most_cols = min(col_tiles, row_blocks.shape[0])
    caps = [level for level in LEVELS if level[0] < most_rows and level[1] < most_cols]
    caps.append((most_rows, most_cols))
    in_row = jnp.sum(row_blocks[None, :] // row_tiles == jnp.arange(n_row)[:, None], axis=1)
    in_col = jnp.sum(row_blocks[None, :] // col_tiles == jnp.arange(n_col)[:, None], axis=1)
    needed_rows, needed_cols = jnp.max(in_row), jnp.max(in_col)
    fits = [(needed_rows <= rows) & (needed_cols <= cols) for rows, cols in caps]
    choice = jnp.argmax(jnp.stack(fits))
    operands = (ancestor_inv, lower_hat, diag_term, row_blocks)
    if len(caps) == 1:
        return level_body(caps[0], *operands)
    return lax.switch(choice, [functools.partial(level_body, level) for level in caps], *operands)


def solution(mesh):
    return jax.shard_map(
        body,
        mesh=mesh,
        in_specs=(
            P(("pole", "row"), "col"),
            P(("pole", "row"), None),
            P(("pole", "row"), ("col", "sub")),
            P(),
        ),
        out_specs=(P(("pole", "row"), ("col", "sub")), P(("pole", "row"), ("col", "sub"))),
        check_vma=False,
    )
```
